128 devices in a mesh: ia: 4 (over x), ja: 8 (over y_lo, z), ka: 4 (over y_hi, core).
Axes of the slice: x: 4, y: 4 (y_hi: 2, y_lo: 2; y = y_hi * 2 + y_lo), z: 4, core: 2. Of those that a mesh axis runs over, the one named last changes fastest.
Arguments:
- tokens: bfloat16 [1536, 6144], P('ja', ('ka', 'ia')), may hold values from -6 to 6
- weight: bfloat16 [6144, 24576], P('ka', ('ia', 'ja')), may hold values from -0.078125 to 0.078125
- grad_out: bfloat16 [1536, 24576], P('ja', ('ia', 'ka')), may hold values from -6 to 6
Outputs:
- activated: bfloat16 [1536, 24576], P('ja', ('ia', 'ka'))
- grad_input: bfloat16 [1536, 6144], P('ja', ('ka', 'ia'))
- grad_weight: bfloat16 [6144, 24576], P('ka', ('ia', 'ja'))
The draws below stay inside these ranges and needn't reach their ends.
All inputs are finite; a program needn't handle non-finite values.
Results may differ from the reference program's by a relative error of at most 0.022.
Values may be sent and summed in bfloat16 or wider, within the bound.
No kernel may reach another device: no remote copies, remote signals or barrier semaphores. Data moves between devices by JAX's collectives and lax.ppermute only.
A program may use at most 128 MiB of HBM per device.

```python
import jax
import jax.numpy as jnp
from jax import lax

D = 6144
FF = 24576
TOK_DEV = 192
TOKENS = 1536
N_JA = 8


def block_levels(stream_key, dims, split, smallest, high):
    def one(position, parts):
        heights = jax.random.uniform(jax.random.fold_in(jax.random.fold_in(stream_key, 6), position), (parts,), jnp.float32, smallest / len(split), high / len(split))
        return jnp.repeat(jnp.exp(heights), dims[position] // parts).reshape((-1,) + (1,) * (len(dims) - position - 1))

    factor_of = one(*split[0])
    for cut in split[1:]:
        factor_of = factor_of * one(*cut)
    return factor_of


def scatter_about(stream_key, shape, deviation, most, cuts=(), held_as=jnp.bfloat16):
    factor_of = block_levels(stream_key, shape, cuts, -0.22, 0.18) if cuts else 1.0
    array = jax.random.normal(stream_key, shape, jnp.float32) * deviation * factor_of
    return jnp.minimum(jnp.maximum(array, -most), most).astype(held_as)


def setup_inputs(seed: int = 0) -> dict:
    key_list = jax.random.split(jax.random.key(seed), 4)
    tokens = scatter_about(key_list[0], (TOKENS, D), 1.0, 6.0, ((0, 8), (1, 16)))
    weight = scatter_about(key_list[1], (D, FF), D ** -0.5, 0.078125, ((0, 4), (1, 32)))
    grad_out = scatter_about(key_list[2], (TOKENS, FF), 1.0, 6.0, ((0, 8), (1, 16)))
    return {"tokens": tokens, "weight": weight, "grad_out": grad_out}


coef_root = 0.7978845608028654
coef_cube = 0.044715


def gelu_pair(hidden):
    tanh_value = jnp.tanh(coef_root * (hidden + coef_cube * hidden * hidden * hidden))
    activ = 0.5 * hidden * (1.0 + tanh_value)
    derivative = 0.5 * (1.0 + tanh_value) + 0.5 * hidden * (1.0 - tanh_value * tanh_value) * coef_root * (1.0 + 3.0 * coef_cube * hidden * hidden)
    return activ, derivative


def reference(tokens, weight, grad_out):
    hidden = jnp.dot(tokens, weight, preferred_element_type=jnp.float32)
    activ, derivative = gelu_pair(hidden)
    activated = activ.astype(jnp.bfloat16)
    grad_hidden = (grad_out.astype(jnp.float32) * derivative).astype(jnp.bfloat16)
    grad_input = lax.dot_general(grad_hidden, weight, (((1,), (1,)), ((), ())), preferred_element_type=jnp.float32).astype(jnp.bfloat16)
    token_groups = tokens.reshape(N_JA, TOK_DEV, D)
    grad_groups = grad_hidden.reshape(N_JA, TOK_DEV, FF)

    def accumulate(carried, pieces):
        group_term = lax.dot_general(pieces[0], pieces[1], (((0,), (0,)), ((), ())), preferred_element_type=jnp.float32).astype(jnp.bfloat16)
        return carried + group_term.astype(jnp.float32), None

    summed, unused = lax.scan(accumulate, jnp.zeros((D, FF), jnp.float32), (token_groups, grad_groups))
    return activated, grad_input, summed.astype(jnp.bfloat16)
```

```python
import jax
import jax.numpy as jnp
from jax import lax
from jax.sharding import PartitionSpec as P

coef_root = 0.7978845608028654
coef_cube = 0.044715
bf16, f32 = jnp.bfloat16, jnp.float32

N_X, N_Z = 4, 4


def gelu_pair(hidden):
    tanh_value = jnp.tanh(coef_root * (hidden + coef_cube * hidden * hidden * hidden))
    activ = 0.5 * hidden * (1.0 + tanh_value)
    derivative = 0.5 * (1.0 + tanh_value) + 0.5 * hidden * (
        1.0 - tanh_value * tanh_value
    ) * coef_root * (1.0 + 3.0 * coef_cube * hidden * hidden)
    return (activ, derivative)


def from_x(v, r):
    return lax.ppermute(v, "ia", [((i + r) % N_X, i) for i in range(N_X)])


def to_x(v, r):
    return from_x(v, N_X - r)


def from_z(v, r):
    return lax.ppermute(
        v, "ja", [(y * N_Z + (z + r) % N_Z, y * N_Z + z) for y in range(2) for z in range(N_Z)]
    )


def to_z(v, r):
    return from_z(v, N_Z - r)


def swap_y_lo(v):
    return lax.ppermute(v, "ja", [(j, (j + N_Z) % (2 * N_Z)) for j in range(2 * N_Z)])


def swap_y_hi(v):
    return lax.ppermute(v, "ka", [(k, (k + 2) % 4) for k in range(4)])


def swap_core(v):
    return lax.ppermute(v, "ka", [(k, k ^ 1) for k in range(4)])


def exchange_pairs(slot):
    pairs = []
    for y_lo in range(2):
        for z in range(N_Z):
            for y_hi in range(2):
                for core in range(2):
                    half = (z + slot) % 2
                    to_z_index = 2 * core + half
                    to_y_lo, to_y_hi = y_hi, y_hi ^ y_lo
                    to_core = ((z - to_z_index) % N_Z) // 2
                    pairs.append(
                        (
                            (y_lo * N_Z + z) * 4 + y_hi * 2 + core,
                            (to_y_lo * N_Z + to_z_index) * 4 + to_y_hi * 2 + to_core,
                        )
                    )
    return pairs


def dot(a, b, dims=(1, 0)):
    return lax.dot_general(
        a, b, (((dims[0],), (dims[1],)), ((), ())), preferred_element_type=f32
    )


def on_device(tokens, weight, grad_out):
    rows, cols = tokens.shape
    half = rows // 2
    units = weight.shape[1]
    x = lax.axis_index("ia")
    z = lax.axis_index("ja") % N_Z
    y_hi, core = lax.axis_index("ka") // 2, lax.axis_index("ka") % 2

    other = swap_y_lo(tokens)
    tok_a = jnp.concatenate([tokens[:half], other[:half]], 0)
    tok_b = jnp.concatenate([tokens[half:], other[half:]], 0)
    a_x = [tok_a] + [from_x(tok_a, r) for r in (1, 2, 3)]
    b_z = [tok_b] + [from_z(tok_b, r) for r in (1, 2, 3)]
    tok_a = jnp.concatenate(a_x, 1)
    tok_b = jnp.concatenate(b_z, 0)
    a_z = [tok_a] + [from_z(tok_a, r) for r in (1, 2, 3)]
    b_x = [tok_b] + [from_x(tok_b, r) for r in (1, 2, 3)]
    tok_a = jnp.concatenate(a_z, 0)
    tok_b = jnp.concatenate(b_x, 1)

    sent = []
    for slot in range(2):
        start = ((z + slot) % 2) * units
        piece = lax.dynamic_slice_in_dim(grad_out, start, units, 1)
        sent.append(lax.ppermute(piece, ("ja", "ka"), exchange_pairs(slot)))

    turned = jnp.concatenate(
        [lax.dynamic_slice_in_dim(weight, ((x + r) % N_X) * cols, cols, 0) for r in range(N_X)], 0
    )

    def middle(tok, go):
        pair = tok.shape[0] // 2
        away = lax.dynamic_slice_in_dim(tok, (1 - core) * pair, pair, 0)
        keep = lax.dynamic_slice_in_dim(tok, core * pair, pair, 0)
        got = swap_core(dot(away, turned).astype(bf16))
        summed = (dot(keep, turned) + got.astype(f32)).reshape(2, 2, half, units)
        away = lax.dynamic_slice_in_dim(summed, 1 - y_hi, 1, 1)[:, 0]
        keep = lax.dynamic_slice_in_dim(summed, y_hi, 1, 1)[:, 0]
        hidden = keep + swap_y_hi(away.astype(bf16)).astype(f32)
        activ, derivative = gelu_pair(hidden)
        grad = (go.astype(f32) * derivative).astype(bf16)
        there = swap_y_hi(grad)
        first = jnp.where(y_hi == 0, grad, there)
        second = jnp.where(y_hi == 0, there, grad)
        grad = jnp.stack([first, second], 1).reshape(pair, units)
        there = swap_core(grad)
        first = jnp.where(core == 0, grad, there)
        second = jnp.where(core == 0, there, grad)
        return activ.astype(bf16), jnp.concatenate([first, second], 0)

    act_a, grad_a = middle(tok_a, jnp.stack([s[:half] for s in sent]))
    act_b, grad_b = middle(tok_b, jnp.stack([s[half:] for s in sent]))

    back = []
    for slot in range(2):
        piece = jnp.concatenate([act_a[slot], act_b[slot]], 0)
        back.append(
            lax.ppermute(piece, ("ja", "ka"), [(t, s) for s, t in exchange_pairs(slot)])
        )
    even = z % 2 == 0
    activated = jnp.concatenate(
        [jnp.where(even, back[0], back[1]), jnp.where(even, back[1], back[0])], 1
    )

    def split_sum(parts, send):
        got = [send(parts[r].astype(bf16), r) for r in (2, 1, 3)]
        total = parts[0]
        for g in got:
            total = total + g.astype(f32)
        return total

    n = grad_a.shape[0] // N_Z
    part_a = split_sum(
        [dot(grad_a[r * n : (r + 1) * n], turned, (1, 1)) for r in range(N_Z)], to_z
    )
    part_b = split_sum(
        [dot(grad_b, turned[r * cols : (r + 1) * cols], (1, 1)) for r in range(N_X)], to_x
    )
    part_a = split_sum([part_a[:, r * cols : (r + 1) * cols] for r in range(N_X)], to_x)
    part_b = split_sum([part_b[r * n : (r + 1) * n] for r in range(N_Z)], to_z)
    got = swap_y_lo(jnp.concatenate([part_a[half:], part_b[half:]], 0).astype(bf16))
    grad_input = jnp.concatenate([part_a[:half], part_b[:half]], 0) + got.astype(f32)

    grad_weight = jnp.zeros_like(weight)
    for r in range(N_X):
        block = dot(tok_a[:, r * cols : (r + 1) * cols], grad_a, (0, 0)) + dot(
            tok_b[:, r * cols : (r + 1) * cols], grad_b, (0, 0)
        )
        grad_weight = lax.dynamic_update_slice_in_dim(
            grad_weight, block.astype(bf16), ((x + r) % N_X) * cols, 0
        )
    return (activated, grad_input.astype(bf16), grad_weight)


def solution(mesh):
    placed = (P("ja", ("ka", "ia")), P("ka", ("ia", "ja")), P("ja", ("ia", "ka")))
    return jax.shard_map(
        on_device,
        mesh=mesh,
        in_specs=placed,
        out_specs=(P("ja", ("ia", "ka")), P("ja", ("ka", "ia")), P("ka", ("ia", "ja"))),
        check_vma=False,
    )
```

```python
import jax
import jax.numpy as jnp
from jax import lax
from jax.sharding import PartitionSpec as P

coef_root = 0.7978845608028654
coef_cube = 0.044715
bf16, f32 = jnp.bfloat16, jnp.float32

N_RING = 4
BOTH = ("ja", "ka")


def gelu_pair(hidden):
    tanh_value = jnp.tanh(coef_root * (hidden + coef_cube * hidden * hidden * hidden))
    activ = 0.5 * hidden * (1.0 + tanh_value)
    derivative = 0.5 * (1.0 + tanh_value) + 0.5 * hidden * (
        1.0 - tanh_value * tanh_value
    ) * coef_root * (1.0 + 3.0 * coef_cube * hidden * hidden)
    return (activ, derivative)


def from_x(v, r):
    return lax.ppermute(v, "ia", [((i + r) % N_RING, i) for i in range(N_RING)])


def to_x(v, r):
    return from_x(v, N_RING - r)


def from_z(v, r):
    return lax.ppermute(
        v, "ja", [(y * 4 + (z + r) % N_RING, y * 4 + z) for y in range(2) for z in range(N_RING)]
    )


def to_z(v, r):
    return from_z(v, N_RING - r)


def swap_y_lo(v):
    return lax.ppermute(v, "ja", [(j, j ^ 4) for j in range(8)])


def swap_y_hi(v):
    return lax.ppermute(v, "ka", [(k, k ^ 2) for k in range(4)])


def swap_core(v):
    return lax.ppermute(v, "ka", [(k, k ^ 1) for k in range(4)])


def exchange_pairs(turn):
    pairs = []
    for y_lo in range(2):
        for z in range(4):
            for y_hi in range(2):
                for core in range(2):
                    half = turn ^ (z // 2)
                    to_ja = y_hi * 4 + 2 * core + half
                    to_ka = (y_hi ^ y_lo) * 2 + ((z % 2) ^ half)
                    pairs.append(((y_lo * 4 + z) * 4 + y_hi * 2 + core, to_ja * 4 + to_ka))
    return pairs


def dot(a, b, dims=(1, 0)):
    return lax.dot_general(
        a, b, (((dims[0],), (dims[1],)), ((), ())), preferred_element_type=f32
    )


def after_done(v, *arrived):
    return lax.optimization_barrier((v, *arrived))[0]


def pick(index, first, second):
    return jnp.where(index == 0, first, second)


def on_device(tokens, weight, grad_out):
    rows, cols = tokens.shape
    half = rows // 2
    units = weight.shape[1]
    x = lax.axis_index("ia")
    z = lax.axis_index("ja") % 4
    z_hi, z_lo = z // 2, z % 2
    y_hi, core = lax.axis_index("ka") // 2, lax.axis_index("ka") % 2

    left, right = grad_out[:, :units], grad_out[:, units:]
    piece0, piece1 = pick(z_hi, left, right), pick(z_hi, right, left)

    other = swap_y_lo(tokens)
    sent0 = lax.ppermute(piece0, BOTH, exchange_pairs(0))
    sent1 = lax.ppermute(after_done(piece1, other), BOTH, exchange_pairs(1))
    tok_a = jnp.concatenate([tokens[:half], other[:half]], 0)
    tok_b = jnp.concatenate([tokens[half:], other[half:]], 0)
    b2, b1, b3 = (from_z(tok_b, r) for r in (2, 1, 3))
    a2, a1, a3 = (from_x(tok_a, r) for r in (2, 1, 3))
    a0 = jnp.concatenate([tok_a, a1, a2, a3], 1)
    b0 = jnp.concatenate([tok_b, b2, b1, b3], 0)
    n = 2 * half

    held = after_done(weight, a0, b0)
    w = [lax.dynamic_slice_in_dim(held, ((x + r) % N_RING) * cols, cols, 0) for r in range(4)]
    turned = jnp.concatenate(w, 0)
    w = [turned[r * cols : (r + 1) * cols] for r in range(4)]

    a0, b0 = after_done(a0, sent0), after_done(b0, sent0)
    a1, a3 = from_z(a0, 1), from_z(a0, 3)
    b1, b3 = from_x(b0, 1), from_x(b0, 3)
    a2 = jnp.concatenate([from_z(a1[:half], 1), from_z(a3[half:], 3)], 0)
    b2_first, b2_second = from_x(b1[: 2 * n], 1), from_x(b3[2 * n :], 3)

    def middle(of_core, go):
        first, second = of_core
        got = swap_core(pick(core, second, first).astype(bf16))
        summed = (pick(core, first, second) + got.astype(f32)).reshape(-1, 2, half, units)
        got = swap_y_hi(pick(y_hi, summed[:, 1], summed[:, 0]).astype(bf16))
        hidden = pick(y_hi, summed[:, 0], summed[:, 1]) + got.astype(f32)
        activ, derivative = gelu_pair(hidden)
        grad = (go.reshape(hidden.shape).astype(f32) * derivative).astype(bf16)
        return activ.astype(bf16), grad

    def regroup(grad):
        there = swap_y_hi(grad)
        grad = jnp.stack([pick(y_hi, grad, there), pick(y_hi, there, grad)], 1)
        there = swap_core(grad)
        return (
            pick(core, grad, there).reshape(-1, units),
            pick(core, there, grad).reshape(-1, units),
        )

    k0 = z_lo ^ z_hi ^ (core & z_lo)
    go0, go1 = pick(k0, sent0, sent1), pick(k0, sent1, sent0)

    act_e, gr_e = middle((dot(a0, turned), dot(a1, turned)), go0[:half])
    act_l, gr_l = middle((dot(a2, turned), dot(a3, turned)), go1[:half])
    early = dot(b0, w[0]) + dot(b1, w[1]) + dot(b3, w[3])
    act_b, gr_b = middle(
        (early[: 2 * n] + dot(b2_first, w[2]), early[2 * n :] + dot(b2_second, w[2])),
        jnp.stack([go0[half:], go1[half:]]),
    )

    g2, g3 = regroup(gr_l)
    gb0, gb1 = regroup(gr_b)
    g0, g1 = regroup(gr_e)

    d2 = dot(g2, turned, (1, 1)).astype(bf16)
    c2_first, c2_second = dot(gb0, w[2], (1, 1)).astype(bf16), dot(gb1, w[2], (1, 1)).astype(bf16)
    up_a, down_a = to_z(d2[:half], 1), to_z(d2[half:], 3)
    up_b, down_b = to_x(c2_first, 1), to_x(c2_second, 3)
    up_a, down_a, up_b, down_b = lax.optimization_barrier((up_a, down_a, up_b, down_b))

    held0 = jnp.concatenate([act_e[0], act_b[0]], 0)
    held1 = jnp.concatenate([act_l[0], act_b[1]], 0)

    def give_back(turn, *arrived):
        piece = after_done(pick(k0 ^ turn, held0, held1), *arrived)
        return lax.ppermute(piece, BOTH, [(t, s) for s, t in exchange_pairs(turn)])

    back0 = give_back(0, up_a, up_b)

    def before(v, extra):
        return jnp.pad(v, ((0, extra), (0, 0))).astype(f32)

    def after(v, extra):
        return jnp.pad(v, ((extra, 0), (0, 0))).astype(f32)

    gb = jnp.concatenate([gb0, gb1], 0)
    d1 = (dot(g1, turned, (1, 1)) + before(up_a, half)).astype(bf16)
    d3 = (dot(g3, turned, (1, 1)) + after(down_a, half)).astype(bf16)
    c1 = (dot(gb, w[1], (1, 1)) + before(up_b, 2 * n)).astype(bf16)
    c3 = (dot(gb, w[3], (1, 1)) + after(down_b, 2 * n)).astype(bf16)
    d1, d3, c1, c3 = to_z(d1, 1), to_z(d3, 3), to_x(c1, 1), to_x(c3, 3)
    back1 = give_back(1, d1, c1)
    part_a = dot(g0, turned, (1, 1)) + d1.astype(f32) + d3.astype(f32)
    part_b = dot(gb, w[0], (1, 1)) + c1.astype(f32) + c3.astype(f32)

    part_a = after_done(part_a, back0)

    def split_sum(parts, send):
        got = {r: send(parts[r].astype(bf16), r) for r in (2, 1, 3)}
        return parts[0] + got[1].astype(f32) + got[2].astype(f32) + got[3].astype(f32)

    part_a = split_sum([part_a[:, r * cols : (r + 1) * cols] for r in range(4)], to_x)
    part_b = split_sum([part_b[i * n : (i + 1) * n] for i in (0, 2, 1, 3)], to_z)
    got = swap_y_lo(jnp.concatenate([part_a[half:], part_b[half:]], 0).astype(bf16))
    grad_input = jnp.concatenate([part_a[:half], part_b[:half]], 0) + got.astype(f32)

    activated = jnp.concatenate([pick(z_hi, back0, back1), pick(z_hi, back1, back0)], 1)

    ga = after_done(jnp.concatenate([g0, g1, g2, g3], 0), up_a, up_b)
    gb = after_done(gb, up_a, up_b)
    all_a = jnp.concatenate([a0, a1, a2, a3], 0)
    b2 = jnp.concatenate([b2_first, b2_second], 0)
    grad_weight = jnp.zeros_like(weight)
    for r, b in enumerate((b0, b1, b2, b3)):
        block = dot(all_a[:, r * cols : (r + 1) * cols], ga, (0, 0)) + dot(b, gb, (0, 0))
        grad_weight = lax.dynamic_update_slice_in_dim(
            grad_weight, block.astype(bf16), ((x + r) % N_RING) * cols, 0
        )
    return (activated, grad_input.astype(bf16), grad_weight)


def solution(mesh):
    placed = (P("ja", ("ka", "ia")), P("ka", ("ia", "ja")), P("ja", ("ia", "ka")))
    return jax.shard_map(
        on_device,
        mesh=mesh,
        in_specs=placed,
        out_specs=(P("ja", ("ia", "ka")), P("ja", ("ka", "ia")), P("ka", ("ia", "ja"))),
        check_vma=False,
    )
```

```python
import jax
import jax.numpy as jnp
from jax import lax
from jax.sharding import PartitionSpec as P

coef_root = 0.7978845608028654
coef_cube = 0.044715
bf16, f32 = jnp.bfloat16, jnp.float32

N_RING = 4
BOTH = ("ja", "ka")


def gelu_pair(hidden):
    tanh_value = jnp.tanh(coef_root * (hidden + coef_cube * hidden * hidden * hidden))
    activ = 0.5 * hidden * (1.0 + tanh_value)
    derivative = 0.5 * (1.0 + tanh_value) + 0.5 * hidden * (
        1.0 - tanh_value * tanh_value
    ) * coef_root * (1.0 + 3.0 * coef_cube * hidden * hidden)
    return (activ, derivative)


def from_x(v, r):
    return lax.ppermute(v, "ia", [((i + r) % N_RING, i) for i in range(N_RING)])


def to_x(v, r):
    return from_x(v, N_RING - r)


def from_z(v, r):
    return lax.ppermute(
        v, "ja", [(y * 4 + (z + r) % N_RING, y * 4 + z) for y in range(2) for z in range(N_RING)]
    )


def to_z(v, r):
    return from_z(v, N_RING - r)


def swap_y_lo(v):
    return lax.ppermute(v, "ja", [(j, j ^ 4) for j in range(8)])


def swap_y_hi(v):
    return lax.ppermute(v, "ka", [(k, k ^ 2) for k in range(4)])


def swap_core(v):
    return lax.ppermute(v, "ka", [(k, k ^ 1) for k in range(4)])


def exchange_pairs(turn):
    pairs = []
    for y_lo in range(2):
        for z in range(4):
            for y_hi in range(2):
                for core in range(2):
                    half = turn ^ (z // 2)
                    to_ja = y_hi * 4 + 2 * core + half
                    to_ka = (y_hi ^ y_lo ^ core) * 2 + ((z % 2) ^ half)
                    pairs.append(((y_lo * 4 + z) * 4 + y_hi * 2 + core, to_ja * 4 + to_ka))
    return pairs


def dot(a, b, dims=(1, 0)):
    return lax.dot_general(
        a, b, (((dims[0],), (dims[1],)), ((), ())), preferred_element_type=f32
    )


def after_done(v, *arrived):
    return lax.optimization_barrier((v, *arrived))[0]


def together(*arrays):
    return lax.optimization_barrier(arrays)


def pick(index, first, second):
    return jnp.where(index == 0, first, second)


def on_device(tokens, weight, grad_out):
    rows, cols = tokens.shape
    half = rows // 2
    units = weight.shape[1]
    x = lax.axis_index("ia")
    z = lax.axis_index("ja") % 4
    z_hi, z_lo = z // 2, z % 2
    y_hi, core = lax.axis_index("ka") // 2, lax.axis_index("ka") % 2
    y_rows = y_hi ^ z_hi

    left, right = grad_out[:, :units], grad_out[:, units:]
    piece0, piece1 = pick(z_hi, left, right), pick(z_hi, right, left)

    other = swap_y_lo(tokens)
    tok_a = jnp.concatenate([tokens[:half], other[:half]], 0)
    tok_b = jnp.concatenate([tokens[half:], other[half:]], 0)
    b2, b1, b3 = (from_z(tok_b, r) for r in (2, 1, 3))
    a2, a1, a3 = (from_x(tok_a, r) for r in (2, 1, 3))
    a1, a2, a3, b1, b2, b3 = together(a1, a2, a3, b1, b2, b3)
    a0 = jnp.concatenate([tok_a, a1, a2, a3], 1)
    b0 = jnp.concatenate([tok_b, b2, b1, b3], 0)
    n = 2 * half

    held = after_done(weight, a0, b0)
    w = [lax.dynamic_slice_in_dim(held, ((x + r) % N_RING) * cols, cols, 0) for r in range(4)]
    turned = jnp.concatenate(w, 0)
    w = [turned[r * cols : (r + 1) * cols] for r in range(4)]

    sent0 = lax.ppermute(after_done(piece0, a0, b0), BOTH, exchange_pairs(0))
    a1, a3 = from_z(a0, 1), from_z(a0, 3)
    b1, b3 = from_x(b0, 1), from_x(b0, 3)
    a1, a3, b1, b3, sent0 = together(a1, a3, b1, b3, sent0)
    a2_first, a2_second = from_z(a1[:half], 1), from_z(a3[half:], 3)
    b2_first, b2_second = from_x(b1[: 2 * n], 1), from_x(b3[2 * n :], 3)
    early = dot(b0, w[0]) + dot(b1, w[1]) + dot(b3, w[3])
    sent1 = lax.ppermute(after_done(piece1, early), BOTH, exchange_pairs(1))
    a2_first, a2_second, b2_first, b2_second, sent1 = together(
        a2_first, a2_second, b2_first, b2_second, sent1
    )
    a2 = jnp.concatenate([a2_first, a2_second], 0)

    def over_core(first, second):
        got = swap_core(pick(core, second, first).astype(bf16))
        return (pick(core, first, second) + got.astype(f32)).reshape(-1, 2, half, units)

    def over_y(summed, *arrived):
        away = after_done(pick(y_rows, summed[:, 1], summed[:, 0]).astype(bf16), *arrived)
        return pick(y_rows, summed[:, 0], summed[:, 1]) + swap_y_hi(away).astype(f32)

    def gelu(hidden, go):
        activ, derivative = gelu_pair(hidden)
        grad = (go.reshape(hidden.shape).astype(f32) * derivative).astype(bf16)
        return activ.astype(bf16), grad

    def back_core(grad, there):
        grad = jnp.concatenate(
            [v[i] for i in range(grad.shape[0]) for v in (pick(y_rows, grad, there), pick(y_rows, there, grad))], 0
        )
        there = swap_core(grad)
        return pick(core, grad, there), pick(core, there, grad)

    k0 = z_lo ^ z_hi ^ (core & z_lo)
    go0, go1 = pick(k0, sent0, sent1), pick(k0, sent1, sent0)

    first, second = [dot(a0, turned), dot(a2, turned)], [dot(a1, turned), dot(a3, turned)]
    summed_a = over_core(jnp.concatenate(first, 0), jnp.concatenate(second, 0))
    summed_b = over_core(
        early[: 2 * n] + dot(b2_first, w[2]), early[2 * n :] + dot(b2_second, w[2])
    )
    hidden_a, hidden_b = over_y(summed_a), over_y(summed_b)
    act_a, gr_a = gelu(hidden_a, jnp.concatenate([go0[:half], go1[:half]], 0))
    act_b, gr_b = gelu(hidden_b, jnp.concatenate([go0[half:], go1[half:]], 0))
    there_a, there_b = swap_y_hi(gr_a), swap_y_hi(gr_b)

    first, second = back_core(gr_a, there_a)
    g0, g2, g1, g3 = first[:n], first[n:], second[:n], second[n:]
    gb0, gb1 = back_core(gr_b, there_b)

    d2 = dot(g2, turned, (1, 1)).astype(bf16)
    c2_first, c2_second = dot(gb0, w[2], (1, 1)).astype(bf16), dot(gb1, w[2], (1, 1)).astype(bf16)
    up_a, down_a = to_z(d2[:half], 1), to_z(d2[half:], 3)
    up_b, down_b = to_x(c2_first, 1), to_x(c2_second, 3)

    def before(v, extra):
        return jnp.pad(v, ((0, extra), (0, 0))).astype(f32)

    def after(v, extra):
        return jnp.pad(v, ((extra, 0), (0, 0))).astype(f32)

    gb = jnp.concatenate(together(gb0, gb1, d2, c2_first, c2_second)[:2], 0)
    held0 = jnp.concatenate([act_a[0], act_b[0]], 0)
    held1 = jnp.concatenate([act_a[1], act_b[1]], 0)

    def give_back(turn, *arrived):
        piece = after_done(pick(k0 ^ turn, held0, held1), *arrived)
        return lax.ppermute(piece, BOTH, [(t, s) for s, t in exchange_pairs(turn)])

    back0 = give_back(0, d2, c2_first, c2_second)
    up_a, down_a, up_b, down_b, back0 = together(up_a, down_a, up_b, down_b, back0)
    d1 = (dot(g1, turned, (1, 1)) + before(up_a, half)).astype(bf16)
    d3 = (dot(g3, turned, (1, 1)) + after(down_a, half)).astype(bf16)
    c1 = (dot(gb, w[1], (1, 1)) + before(up_b, 2 * n)).astype(bf16)
    c3 = (dot(gb, w[3], (1, 1)) + after(down_b, 2 * n)).astype(bf16)
    added = (d1, d3, c1, c3)
    d1, d3, c1, c3 = to_z(d1, 1), to_z(d3, 3), to_x(c1, 1), to_x(c3, 3)
    d1, d3, c1, c3 = together(d1, d3, c1, c3)
    part_a = dot(g0, turned, (1, 1)) + d1.astype(f32) + d3.astype(f32)
    part_b = dot(gb, w[0], (1, 1)) + c1.astype(f32) + c3.astype(f32)

    ga = after_done(jnp.concatenate([g0, g1, g2, g3], 0), *added)
    gb = after_done(gb, d1, c1)
    all_a = jnp.concatenate([a0, a1, a2, a3], 0)
    b2 = jnp.concatenate([b2_first, b2_second], 0)
    blocks = []
    for r, b in enumerate((b0, b1, b2, b3)):
        block = dot(all_a[:, r * cols : (r + 1) * cols], ga, (0, 0)) + dot(b, gb, (0, 0))
        blocks.append(block.astype(bf16))

    back1 = give_back(1, *added)
    grad_weight = jnp.zeros_like(weight)
    for r in range(4):
        grad_weight = lax.dynamic_update_slice_in_dim(
            grad_weight, blocks[r], ((x + r) % N_RING) * cols, 0
        )

    part_a, part_b, back1 = together(part_a, part_b, back1)

    def split_sum(parts, send):
        got = {r: send(parts[r].astype(bf16), r) for r in (2, 1, 3)}
        return parts[0] + got[1].astype(f32) + got[2].astype(f32) + got[3].astype(f32)

    part_a = split_sum([part_a[:, r * cols : (r + 1) * cols] for r in range(4)], to_x)
    part_b = split_sum([part_b[i * n : (i + 1) * n] for i in (0, 2, 1, 3)], to_z)
    got = swap_y_lo(jnp.concatenate([part_a[half:], part_b[half:]], 0).astype(bf16))
    grad_input = jnp.concatenate([part_a[:half], part_b[:half]], 0) + got.astype(f32)

    activated = jnp.concatenate([pick(z_hi, back0, back1), pick(z_hi, back1, back0)], 1)

    return (activated, grad_input.astype(bf16), grad_weight)


def solution(mesh):
    placed = (P("ja", ("ka", "ia")), P("ka", ("ia", "ja")), P("ja", ("ia", "ka")))
    return jax.shard_map(
        on_device,
        mesh=mesh,
        in_specs=placed,
        out_specs=(P("ja", ("ia", "ka")), P("ja", ("ka", "ia")), P("ka", ("ia", "ja"))),
        check_vma=False,
    )
```

```python
import jax
import jax.numpy as jnp
from jax import lax
from jax.sharding import PartitionSpec as P

coef_root = 0.7978845608028654
coef_cube = 0.044715
bf16, f32 = jnp.bfloat16, jnp.float32

N_RING = 4
BOTH = ("ja", "ka")


def gelu_pair(hidden):
    tanh_value = jnp.tanh(coef_root * (hidden + coef_cube * hidden * hidden * hidden))
    activ = 0.5 * hidden * (1.0 + tanh_value)
    derivative = 0.5 * (1.0 + tanh_value) + 0.5 * hidden * (
        1.0 - tanh_value * tanh_value
    ) * coef_root * (1.0 + 3.0 * coef_cube * hidden * hidden)
    return (activ, derivative)


def from_x(v, r):
    return lax.ppermute(v, "ia", [((i + r) % N_RING, i) for i in range(N_RING)])


def to_x(v, r):
    return from_x(v, N_RING - r)


def from_z(v, r):
    return lax.ppermute(
        v, "ja", [(y * 4 + (z + r) % N_RING, y * 4 + z) for y in range(2) for z in range(N_RING)]
    )


def to_z(v, r):
    return from_z(v, N_RING - r)


def swap_y_lo(v):
    return lax.ppermute(v, "ja", [(j, j ^ 4) for j in range(8)])


def swap_y_hi(v):
    return lax.ppermute(v, "ka", [(k, k ^ 2) for k in range(4)])


def swap_core(v):
    return lax.ppermute(v, "ka", [(k, k ^ 1) for k in range(4)])


def exchange_pairs(turn):
    pairs = []
    for y_lo in range(2):
        for z in range(4):
            for y_hi in range(2):
                for core in range(2):
                    half = turn ^ (z // 2)
                    to_ja = y_hi * 4 + 2 * core + half
                    to_ka = (y_hi ^ y_lo ^ core) * 2 + ((z % 2) ^ half)
                    pairs.append(((y_lo * 4 + z) * 4 + y_hi * 2 + core, to_ja * 4 + to_ka))
    return pairs


def dot(a, b, dims=(1, 0)):
    return lax.dot_general(
        a, b, (((dims[0],), (dims[1],)), ((), ())), preferred_element_type=f32
    )


def after_done(v, *arrived):
    return lax.optimization_barrier((v, *arrived))[0]


def together(*arrays):
    return lax.optimization_barrier(arrays)


def pick(index, first, second):
    return jnp.where(index == 0, first, second)


def on_device(tokens, weight, grad_out):
    rows, cols = tokens.shape
    half = rows // 2
    units = weight.shape[1]
    x = lax.axis_index("ia")
    z = lax.axis_index("ja") % 4
    z_hi, z_lo = z // 2, z % 2
    y_hi, core = lax.axis_index("ka") // 2, lax.axis_index("ka") % 2
    y_rows = y_hi ^ z_hi

    left, right = grad_out[:, :units], grad_out[:, units:]
    piece0, piece1 = pick(z_hi, left, right), pick(z_hi, right, left)

    other = swap_y_lo(tokens)
    tok_a = jnp.concatenate([tokens[:half], other[:half]], 0)
    tok_b = jnp.concatenate([tokens[half:], other[half:]], 0)
    b2, b1, b3 = (from_z(tok_b, r) for r in (2, 1, 3))
    a2, a1, a3 = (from_x(tok_a, r) for r in (2, 1, 3))
    a0 = jnp.concatenate([tok_a, a1, a2, a3], 1)
    b0 = jnp.concatenate([tok_b, b2, b1, b3], 0)
    n = 2 * half

    held = after_done(weight, a0, b0)
    w = [lax.dynamic_slice_in_dim(held, ((x + r) % N_RING) * cols, cols, 0) for r in range(4)]
    turned = jnp.concatenate(w, 0)
    w = [turned[r * cols : (r + 1) * cols] for r in range(4)]

    sent0 = lax.ppermute(after_done(piece0, a0, b0), BOTH, exchange_pairs(0))
    a1, a3 = from_z(a0, 1), from_z(a0, 3)
    b1, b3 = from_x(b0, 1), from_x(b0, 3)
    a1, a3, b1, b3, sent0 = together(a1, a3, b1, b3, sent0)
    a2_first, a2_second = from_z(a1[:half], 1), from_z(a3[half:], 3)
    b2_first, b2_second = from_x(b1[: 2 * n], 1), from_x(b3[2 * n :], 3)
    early = dot(b0, w[0]) + dot(b1, w[1]) + dot(b3, w[3])
    at_1 = dot(a1, turned)
    sent1 = lax.ppermute(after_done(piece1, early, at_1), BOTH, exchange_pairs(1))
    a2 = jnp.concatenate([a2_first, a2_second], 0)

    def over_core(first, second):
        got = swap_core(pick(core, second, first).astype(bf16))
        return (pick(core, first, second) + got.astype(f32)).reshape(-1, 2, half, units)

    def over_y(summed, *arrived):
        away = after_done(pick(y_rows, summed[:, 1], summed[:, 0]).astype(bf16), *arrived)
        return pick(y_rows, summed[:, 0], summed[:, 1]) + swap_y_hi(away).astype(f32)

    def gelu(hidden, go):
        activ, derivative = gelu_pair(hidden)
        grad = (go.reshape(hidden.shape).astype(f32) * derivative).astype(bf16)
        return activ.astype(bf16), grad

    def back_core(grad, there):
        grad = jnp.concatenate(
            [v[i] for i in range(grad.shape[0]) for v in (pick(y_rows, grad, there), pick(y_rows, there, grad))], 0
        )
        there = swap_core(grad)
        return pick(core, grad, there), pick(core, there, grad)

    first, second = [dot(a0, turned), dot(a2, turned)], [at_1, dot(a3, turned)]
    summed_a = over_core(jnp.concatenate(first, 0), jnp.concatenate(second, 0))
    summed_b = over_core(
        early[: 2 * n] + dot(b2_first, w[2]), early[2 * n :] + dot(b2_second, w[2])
    )
    summed_a, sent1 = together(summed_a, sent1)
    hidden_a, hidden_b = over_y(summed_a), over_y(summed_b)
    k0 = z_lo ^ z_hi ^ (core & z_lo)
    go0, go1 = pick(k0, sent0, sent1), pick(k0, sent1, sent0)
    act_a, gr_a = gelu(hidden_a, jnp.concatenate([go0[:half], go1[:half]], 0))
    act_b, gr_b = gelu(hidden_b, jnp.concatenate([go0[half:], go1[half:]], 0))
    there_a, there_b = swap_y_hi(gr_a), swap_y_hi(gr_b)

    first, second = back_core(gr_a, there_a)
    g0, g2, g1, g3 = first[:n], first[n:], second[:n], second[n:]
    gb0, gb1 = back_core(gr_b, there_b)

    d2 = dot(g2, turned, (1, 1)).astype(bf16)
    c2_first, c2_second = dot(gb0, w[2], (1, 1)).astype(bf16), dot(gb1, w[2], (1, 1)).astype(bf16)
    up_a, down_a = to_z(d2[:half], 1), to_z(d2[half:], 3)
    up_b, down_b = to_x(c2_first, 1), to_x(c2_second, 3)

    def before(v, extra):
        return jnp.pad(v, ((0, extra), (0, 0))).astype(f32)

    def after(v, extra):
        return jnp.pad(v, ((extra, 0), (0, 0))).astype(f32)

    gb = jnp.concatenate(together(gb0, gb1, d2, c2_first, c2_second)[:2], 0)
    held0 = jnp.concatenate([act_a[0], act_b[0]], 0)
    held1 = jnp.concatenate([act_a[1], act_b[1]], 0)

    def give_back(turn, *arrived):
        piece = after_done(pick(k0 ^ turn, held0, held1), *arrived)
        return lax.ppermute(piece, BOTH, [(t, s) for s, t in exchange_pairs(turn)])

    back0 = give_back(0, d2, c2_first, c2_second)
    up_a, down_a, up_b, down_b, back0 = together(up_a, down_a, up_b, down_b, back0)
    d1 = (dot(g1, turned, (1, 1)) + before(up_a, half)).astype(bf16)
    d3 = (dot(g3, turned, (1, 1)) + after(down_a, half)).astype(bf16)
    c1 = (dot(gb, w[1], (1, 1)) + before(up_b, 2 * n)).astype(bf16)
    c3 = (dot(gb, w[3], (1, 1)) + after(down_b, 2 * n)).astype(bf16)
    added = (d1, d3, c1, c3)
    d1, d3, c1, c3 = to_z(d1, 1), to_z(d3, 3), to_x(c1, 1), to_x(c3, 3)
    d1, d3, c1, c3 = together(d1, d3, c1, c3)
    part_a = dot(g0, turned, (1, 1)) + d1.astype(f32) + d3.astype(f32)
    part_b = dot(gb, w[0], (1, 1)) + c1.astype(f32) + c3.astype(f32)

    ga = after_done(jnp.concatenate([g0, g1, g2, g3], 0), *added)
    gb = after_done(gb, d1, c1)
    all_a = jnp.concatenate([a0, a1, a2, a3], 0)
    b2 = jnp.concatenate([b2_first, b2_second], 0)
    blocks = []
    for r, b in enumerate((b0, b1, b2, b3)):
        block = dot(all_a[:, r * cols : (r + 1) * cols], ga, (0, 0)) + dot(b, gb, (0, 0))
        blocks.append(block.astype(bf16))

    back1 = give_back(1, *added)
    grad_weight = jnp.zeros_like(weight)
    for r in range(4):
        grad_weight = lax.dynamic_update_slice_in_dim(
            grad_weight, blocks[r], ((x + r) % N_RING) * cols, 0
        )

    part_a, part_b, back1 = together(part_a, part_b, back1)

    def split_sum(parts, send):
        got = {r: send(parts[r].astype(bf16), r) for r in (2, 1, 3)}
        return parts[0] + got[1].astype(f32) + got[2].astype(f32) + got[3].astype(f32)

    part_a = split_sum([part_a[:, r * cols : (r + 1) * cols] for r in range(4)], to_x)
    part_b = split_sum([part_b[i * n : (i + 1) * n] for i in (0, 2, 1, 3)], to_z)
    got = swap_y_lo(jnp.concatenate([part_a[half:], part_b[half:]], 0).astype(bf16))
    grad_input = jnp.concatenate([part_a[:half], part_b[:half]], 0) + got.astype(f32)

    activated = jnp.concatenate([pick(z_hi, back0, back1), pick(z_hi, back1, back0)], 1)

    return (activated, grad_input.astype(bf16), grad_weight)


def solution(mesh):
    placed = (P("ja", ("ka", "ia")), P("ka", ("ia", "ja")), P("ja", ("ia", "ka")))
    return jax.shard_map(
        on_device,
        mesh=mesh,
        in_specs=placed,
        out_specs=(P("ja", ("ia", "ka")), P("ja", ("ka", "ia")), P("ka", ("ia", "ja"))),
        check_vma=False,
    )
```

```python
import jax
import jax.numpy as jnp
from jax import lax
from jax.sharding import PartitionSpec as P

coef_root = 0.7978845608028654
coef_cube = 0.044715
bf16, f32 = jnp.bfloat16, jnp.float32

N_RING = 4
BOTH = ("ja", "ka")


def gelu_pair(hidden):
    tanh_value = jnp.tanh(coef_root * (hidden + coef_cube * hidden * hidden * hidden))
    activ = 0.5 * hidden * (1.0 + tanh_value)
    derivative = 0.5 * (1.0 + tanh_value) + 0.5 * hidden * (
        1.0 - tanh_value * tanh_value
    ) * coef_root * (1.0 + 3.0 * coef_cube * hidden * hidden)
    return (activ, derivative)


def from_x(v, r):
    return lax.ppermute(v, "ia", [((i + r) % N_RING, i) for i in range(N_RING)])


def to_x(v, r):
    return from_x(v, N_RING - r)


def from_z(v, r):
    return lax.ppermute(
        v, "ja", [(y * 4 + (z + r) % N_RING, y * 4 + z) for y in range(2) for z in range(N_RING)]
    )


def to_z(v, r):
    return from_z(v, N_RING - r)


def swap_y_lo(v):
    return lax.ppermute(v, "ja", [(j, j ^ 4) for j in range(8)])


def swap_y_hi(v):
    return lax.ppermute(v, "ka", [(k, k ^ 2) for k in range(4)])


def swap_core(v):
    return lax.ppermute(v, "ka", [(k, k ^ 1) for k in range(4)])


def exchange_pairs(turn):
    pairs = []
    for y_lo in range(2):
        for z in range(4):
            for y_hi in range(2):
                for core in range(2):
                    half = turn ^ (z // 2)
                    to_ja = y_hi * 4 + 2 * core + half
                    to_ka = (y_hi ^ y_lo ^ core) * 2 + ((z % 2) ^ half)
                    pairs.append(((y_lo * 4 + z) * 4 + y_hi * 2 + core, to_ja * 4 + to_ka))
    return pairs


def dot(a, b, dims=(1, 0)):
    return lax.dot_general(
        a, b, (((dims[0],), (dims[1],)), ((), ())), preferred_element_type=f32
    )


def after_done(v, *arrived):
    return lax.optimization_barrier((v, *arrived))[0]


def together(*arrays):
    return lax.optimization_barrier(arrays)


def pick(index, first, second):
    return jnp.where(index == 0, first, second)


def on_device(tokens, weight, grad_out):
    rows, cols = tokens.shape
    half = rows // 2
    units = weight.shape[1]
    x = lax.axis_index("ia")
    z = lax.axis_index("ja") % 4
    z_hi, z_lo = z // 2, z % 2
    y_hi, core = lax.axis_index("ka") // 2, lax.axis_index("ka") % 2
    y_rows = y_hi ^ z_hi

    left, right = grad_out[:, :units], grad_out[:, units:]
    piece0, piece1 = pick(z_hi, left, right), pick(z_hi, right, left)

    other = swap_y_lo(tokens)
    tok_a = jnp.concatenate([tokens[:half], other[:half]], 0)
    tok_b = jnp.concatenate([tokens[half:], other[half:]], 0)
    b2, b1, b3 = (from_z(tok_b, r) for r in (2, 1, 3))
    a2, a1, a3 = (from_x(tok_a, r) for r in (2, 1, 3))
    a0 = jnp.concatenate([tok_a, a1, a2, a3], 1)
    b0 = jnp.concatenate([tok_b, b2, b1, b3], 0)
    n = 2 * half

    held = after_done(weight, a0, b0)
    w = [lax.dynamic_slice_in_dim(held, ((x + r) % N_RING) * cols, cols, 0) for r in range(4)]
    turned = jnp.concatenate(w, 0)
    w = [turned[r * cols : (r + 1) * cols] for r in range(4)]

    sent0 = lax.ppermute(after_done(piece0, a0, b0), BOTH, exchange_pairs(0))
    a1, a3 = from_z(a0, 1), from_z(a0, 3)
    b1, b3 = from_x(b0, 1), from_x(b0, 3)
    a1, a3, b1, b3, sent0 = together(a1, a3, b1, b3, sent0)
    a2_first, a2_second = from_z(a1[:half], 1), from_z(a3[half:], 3)
    b2_first, b2_second = from_x(b1[: 2 * n], 1), from_x(b3[2 * n :], 3)
    early = dot(b0, w[0]) + dot(b1, w[1]) + dot(b3, w[3])
    at_1 = dot(a1, turned)
    sent1 = lax.ppermute(after_done(piece1, at_1), BOTH, exchange_pairs(1))
    a2 = jnp.concatenate([a2_first, a2_second], 0)

    def over_core(first, second):
        got = swap_core(pick(core, second, first).astype(bf16))
        return (pick(core, first, second) + got.astype(f32)).reshape(-1, 2, half, units)

    def over_y(summed, *arrived):
        away = after_done(pick(y_rows, summed[:, 1], summed[:, 0]).astype(bf16), *arrived)
        return pick(y_rows, summed[:, 0], summed[:, 1]) + swap_y_hi(away).astype(f32)

    def gelu(hidden, go):
        activ, derivative = gelu_pair(hidden)
        grad = (go.reshape(hidden.shape).astype(f32) * derivative).astype(bf16)
        return activ.astype(bf16), grad

    def back_core(grad, there):
        grad = jnp.concatenate(
            [v[i] for i in range(grad.shape[0]) for v in (pick(y_rows, grad, there), pick(y_rows, there, grad))], 0
        )
        there = swap_core(grad)
        return pick(core, grad, there), pick(core, there, grad)

    first, second = [dot(a0, turned), dot(a2, turned)], [at_1, dot(a3, turned)]
    summed_a = over_core(jnp.concatenate(first, 0), jnp.concatenate(second, 0))
    summed_b = over_core(
        early[: 2 * n] + dot(b2_first, w[2]), early[2 * n :] + dot(b2_second, w[2])
    )
    summed_a, sent1 = together(summed_a, sent1)
    hidden_a, hidden_b = over_y(summed_a), over_y(summed_b)
    k0 = z_lo ^ z_hi ^ (core & z_lo)
    go0, go1 = pick(k0, sent0, sent1), pick(k0, sent1, sent0)
    act_a, gr_a = gelu(hidden_a, jnp.concatenate([go0[:half], go1[:half]], 0))
    act_b, gr_b = gelu(hidden_b, jnp.concatenate([go0[half:], go1[half:]], 0))
    there_a, there_b = swap_y_hi(gr_a), swap_y_hi(gr_b)

    first, second = back_core(gr_a, there_a)
    g0, g2, g1, g3 = first[:n], first[n:], second[:n], second[n:]
    d2 = dot(g2, turned, (1, 1)).astype(bf16)
    gb0, gb1 = back_core(gr_b, after_done(there_b, d2))

    c2_first, c2_second = dot(gb0, w[2], (1, 1)).astype(bf16), dot(gb1, w[2], (1, 1)).astype(bf16)
    up_a, down_a = to_z(d2[:half], 1), to_z(d2[half:], 3)
    up_b, down_b = to_x(c2_first, 1), to_x(c2_second, 3)

    def before(v, extra):
        return jnp.pad(v, ((0, extra), (0, 0))).astype(f32)

    def after(v, extra):
        return jnp.pad(v, ((extra, 0), (0, 0))).astype(f32)

    gb = jnp.concatenate(together(gb0, gb1, d2, c2_first, c2_second)[:2], 0)
    held0 = jnp.concatenate([act_a[0], act_b[0]], 0)
    held1 = jnp.concatenate([act_a[1], act_b[1]], 0)

    def give_back(turn, *arrived):
        piece = after_done(pick(k0 ^ turn, held0, held1), *arrived)
        return lax.ppermute(piece, BOTH, [(t, s) for s, t in exchange_pairs(turn)])

    back0 = give_back(0, d2, c2_first, c2_second)
    up_a, down_a, up_b, down_b = together(up_a, down_a, up_b, down_b)
    d1 = (dot(g1, turned, (1, 1)) + before(up_a, half)).astype(bf16)
    d3 = (dot(g3, turned, (1, 1)) + after(down_a, half)).astype(bf16)
    up_b, down_b, back0 = together(up_b, down_b, back0)
    c1 = (dot(gb, w[1], (1, 1)) + before(up_b, 2 * n)).astype(bf16)
    c3 = (dot(gb, w[3], (1, 1)) + after(down_b, 2 * n)).astype(bf16)
    added = (d1, d3, c1, c3)
    d1, d3, c1, c3 = to_z(d1, 1), to_z(d3, 3), to_x(c1, 1), to_x(c3, 3)
    d1, d3, c1, c3 = together(d1, d3, c1, c3)
    part_a = dot(g0, turned, (1, 1)) + d1.astype(f32) + d3.astype(f32)
    part_b = dot(gb, w[0], (1, 1)) + c1.astype(f32) + c3.astype(f32)

    ga = after_done(jnp.concatenate([g0, g1, g2, g3], 0), *added)
    gb = after_done(gb, d1, c1)
    all_a = jnp.concatenate([a0, a1, a2, a3], 0)
    b2 = jnp.concatenate([b2_first, b2_second], 0)
    of_a = lax.optimization_barrier(dot(all_a, ga, (0, 0)))
    blocks = []
    for r, b in enumerate((b0, b1, b2, b3)):
        block = of_a[r * cols : (r + 1) * cols] + dot(b, gb, (0, 0))
        blocks.append(block.astype(bf16))

    back1 = give_back(1, *added)
    grad_weight = jnp.zeros_like(weight)
    for r in range(4):
        grad_weight = lax.dynamic_update_slice_in_dim(
            grad_weight, blocks[r], ((x + r) % N_RING) * cols, 0
        )

    part_a, part_b, back1 = together(part_a, part_b, back1)

    def split_sum(parts, send):
        got = {r: send(parts[r].astype(bf16), r) for r in (2, 1, 3)}
        return parts[0] + got[1].astype(f32) + got[2].astype(f32) + got[3].astype(f32)

    part_a = split_sum([part_a[:, r * cols : (r + 1) * cols] for r in range(4)], to_x)
    part_b = split_sum([part_b[i * n : (i + 1) * n] for i in (0, 2, 1, 3)], to_z)
    got = swap_y_lo(jnp.concatenate([part_a[half:], part_b[half:]], 0).astype(bf16))
    grad_input = jnp.concatenate([part_a[:half], part_b[:half]], 0) + got.astype(f32)

    activated = jnp.concatenate([pick(z_hi, back0, back1), pick(z_hi, back1, back0)], 1)

    return (activated, grad_input.astype(bf16), grad_weight)


def solution(mesh):
    placed = (P("ja", ("ka", "ia")), P("ka", ("ia", "ja")), P("ja", ("ia", "ka")))
    return jax.shard_map(
        on_device,
        mesh=mesh,
        in_specs=placed,
        out_specs=(P("ja", ("ia", "ka")), P("ja", ("ka", "ia")), P("ka", ("ia", "ja"))),
        check_vma=False,
    )
```

```python
import jax
import jax.numpy as jnp
from jax import lax
from jax.sharding import PartitionSpec as P

coef_root = 0.7978845608028654
coef_cube = 0.044715
bf16, f32 = jnp.bfloat16, jnp.float32

N_RING = 4
BOTH = ("ja", "ka")


def gelu_pair(hidden):
    tanh_value = jnp.tanh(coef_root * (hidden + coef_cube * hidden * hidden * hidden))
    activ = 0.5 * hidden * (1.0 + tanh_value)
    derivative = 0.5 * (1.0 + tanh_value) + 0.5 * hidden * (
        1.0 - tanh_value * tanh_value
    ) * coef_root * (1.0 + 3.0 * coef_cube * hidden * hidden)
    return (activ, derivative)


def from_x(v, r):
    return lax.ppermute(v, "ia", [((i + r) % N_RING, i) for i in range(N_RING)])


def to_x(v, r):
    return from_x(v, N_RING - r)


def from_z(v, r):
    return lax.ppermute(
        v, "ja", [(y * 4 + (z + r) % N_RING, y * 4 + z) for y in range(2) for z in range(N_RING)]
    )


def to_z(v, r):
    return from_z(v, N_RING - r)


def swap_y_lo(v):
    return lax.ppermute(v, "ja", [(j, j ^ 4) for j in range(8)])


def swap_y_hi(v):
    return lax.ppermute(v, "ka", [(k, k ^ 2) for k in range(4)])


def swap_core(v):
    return lax.ppermute(v, "ka", [(k, k ^ 1) for k in range(4)])


def exchange_pairs(turn):
    pairs = []
    for y_lo in range(2):
        for z in range(4):
            for y_hi in range(2):
                for core in range(2):
                    half = turn ^ (z // 2)
                    to_ja = y_hi * 4 + 2 * core + half
                    to_ka = (y_hi ^ y_lo ^ core) * 2 + ((z % 2) ^ half)
                    pairs.append(((y_lo * 4 + z) * 4 + y_hi * 2 + core, to_ja * 4 + to_ka))
    return pairs


def dot(a, b, dims=(1, 0)):
    return lax.dot_general(
        a, b, (((dims[0],), (dims[1],)), ((), ())), preferred_element_type=f32
    )


def after_done(v, *arrived):
    return lax.optimization_barrier((v, *arrived))[0]


def together(*arrays):
    return lax.optimization_barrier(arrays)


def pick(index, first, second):
    return jnp.where(index == 0, first, second)


def on_device(tokens, weight, grad_out):
    rows, cols = tokens.shape
    half = rows // 2
    units = weight.shape[1]
    x = lax.axis_index("ia")
    z = lax.axis_index("ja") % 4
    z_hi, z_lo = z // 2, z % 2
    y_hi, core = lax.axis_index("ka") // 2, lax.axis_index("ka") % 2
    y_rows = y_hi ^ z_hi

    left, right = grad_out[:, :units], grad_out[:, units:]
    piece0, piece1 = pick(z_hi, left, right), pick(z_hi, right, left)

    other = swap_y_lo(tokens)
    tok_a = jnp.concatenate([tokens[:half], other[:half]], 0)
    tok_b = jnp.concatenate([tokens[half:], other[half:]], 0)
    b2, b1, b3 = (from_z(tok_b, r) for r in (2, 1, 3))
    a2, a1, a3 = (from_x(tok_a, r) for r in (2, 1, 3))
    a0 = jnp.concatenate([tok_a, a1, a2, a3], 1)
    b0 = jnp.concatenate([tok_b, b2, b1, b3], 0)
    n = 2 * half

    held = after_done(weight, a0, b0)
    w = [lax.dynamic_slice_in_dim(held, ((x + r) % N_RING) * cols, cols, 0) for r in range(4)]
    turned = jnp.concatenate(w, 0)
    w = [turned[r * cols : (r + 1) * cols] for r in range(4)]

    sent0 = lax.ppermute(after_done(piece0, a0, b0), BOTH, exchange_pairs(0))
    a1, a3 = from_z(a0, 1), from_z(a0, 3)
    b1, b3 = from_x(b0, 1), from_x(b0, 3)
    a1, a3, b1, b3, sent0 = together(a1, a3, b1, b3, sent0)
    a2_first, a2_second = from_z(a1[:half], 1), from_z(a3[half:], 3)
    b2_first, b2_second = from_x(b1[: 2 * n], 1), from_x(b3[2 * n :], 3)
    early = dot(b0, w[0]) + dot(b1, w[1]) + dot(b3, w[3])
    at_1 = dot(a1, turned)
    sent1 = lax.ppermute(after_done(piece1, at_1), BOTH, exchange_pairs(1))
    a2 = jnp.concatenate([a2_first, a2_second], 0)

    def over_core(first, second):
        got = swap_core(pick(core, second, first).astype(bf16))
        return (pick(core, first, second) + got.astype(f32)).reshape(-1, 2, half, units)

    def over_y(summed, *arrived):
        away = after_done(pick(y_rows, summed[:, 1], summed[:, 0]).astype(bf16), *arrived)
        return pick(y_rows, summed[:, 0], summed[:, 1]) + swap_y_hi(away).astype(f32)

    def gelu(hidden, go):
        activ, derivative = gelu_pair(hidden)
        grad = (go.reshape(hidden.shape).astype(f32) * derivative).astype(bf16)
        return activ.astype(bf16), grad

    def back_core(grad, there):
        grad = jnp.concatenate(
            [v[i] for i in range(grad.shape[0]) for v in (pick(y_rows, grad, there), pick(y_rows, there, grad))], 0
        )
        there = swap_core(grad)
        return pick(core, grad, there), pick(core, there, grad)

    first, second = [dot(a0, turned), dot(a2, turned)], [at_1, dot(a3, turned)]
    summed_a = over_core(jnp.concatenate(first, 0), jnp.concatenate(second, 0))
    summed_b = over_core(
        early[: 2 * n] + dot(b2_first, w[2]), early[2 * n :] + dot(b2_second, w[2])
    )
    summed_a, sent1 = together(summed_a, sent1)
    hidden_a, hidden_b = over_y(summed_a), over_y(summed_b)
    k0 = z_lo ^ z_hi ^ (core & z_lo)
    go0, go1 = pick(k0, sent0, sent1), pick(k0, sent1, sent0)
    act_a, gr_a = gelu(hidden_a, jnp.concatenate([go0[:half], go1[:half]], 0))
    act_b, gr_b = gelu(hidden_b, jnp.concatenate([go0[half:], go1[half:]], 0))
    there_a, there_b = swap_y_hi(gr_a), swap_y_hi(gr_b)

    first, second = back_core(gr_a, there_a)
    g0, g2, g1, g3 = first[:n], first[n:], second[:n], second[n:]
    d2 = dot(g2, turned, (1, 1)).astype(bf16)
    gb0, gb1 = back_core(gr_b, after_done(there_b, d2))

    c2_first, c2_second = dot(gb0, w[2], (1, 1)).astype(bf16), dot(gb1, w[2], (1, 1)).astype(bf16)
    up_a, down_a = to_z(d2[:half], 1), to_z(d2[half:], 3)
    up_b, down_b = to_x(c2_first, 1), to_x(c2_second, 3)

    def before(v, extra):
        return jnp.pad(v, ((0, extra), (0, 0))).astype(f32)

    def after(v, extra):
        return jnp.pad(v, ((extra, 0), (0, 0))).astype(f32)

    gb = jnp.concatenate(together(gb0, gb1, d2, c2_first, c2_second)[:2], 0)
    held0 = jnp.concatenate([act_a[0], act_b[0]], 0)
    held1 = jnp.concatenate([act_a[1], act_b[1]], 0)

    def give_back(turn, *arrived):
        piece = after_done(pick(k0 ^ turn, held0, held1), *arrived)
        return lax.ppermute(piece, BOTH, [(t, s) for s, t in exchange_pairs(turn)])

    back0 = give_back(0, d2, c2_first, c2_second)
    up_a, down_a, up_b, down_b = together(up_a, down_a, up_b, down_b)
    p1, p3 = together(dot(g1, turned, (1, 1)), dot(g3, turned, (1, 1)))
    d1 = (p1 + before(up_a, half)).astype(bf16)
    d3 = (p3 + after(down_a, half)).astype(bf16)
    up_b, down_b, back0 = together(up_b, down_b, back0)
    q1, q3 = together(dot(gb, w[1], (1, 1)), dot(gb, w[3], (1, 1)))
    c1 = (q1 + before(up_b, 2 * n)).astype(bf16)
    c3 = (q3 + after(down_b, 2 * n)).astype(bf16)
    added = (d1, d3, c1, c3)
    d1, d3, c1, c3 = to_z(d1, 1), to_z(d3, 3), to_x(c1, 1), to_x(c3, 3)
    d1, d3, c1, c3 = together(d1, d3, c1, c3)
    part_a = dot(g0, turned, (1, 1)) + d1.astype(f32) + d3.astype(f32)
    part_b = dot(gb, w[0], (1, 1)) + c1.astype(f32) + c3.astype(f32)

    ga = after_done(jnp.concatenate([g0, g1, g2, g3], 0), *added)
    gb = after_done(gb, d1, c1)
    all_a = jnp.concatenate([a0, a1, a2, a3], 0)
    b2 = jnp.concatenate([b2_first, b2_second], 0)
    of_a = lax.optimization_barrier(dot(all_a, ga, (0, 0)))
    blocks = []
    for r, b in enumerate((b0, b1, b2, b3)):
        block = of_a[r * cols : (r + 1) * cols] + dot(b, gb, (0, 0))
        blocks.append(block.astype(bf16))

    back1 = give_back(1, *added)
    grad_weight = jnp.zeros_like(weight)
    for r in range(4):
        grad_weight = lax.dynamic_update_slice_in_dim(
            grad_weight, blocks[r], ((x + r) % N_RING) * cols, 0
        )

    part_a, part_b, back1 = together(part_a, part_b, back1)

    def split_sum(parts, send):
        got = {r: send(parts[r].astype(bf16), r) for r in (2, 1, 3)}
        return parts[0] + got[1].astype(f32) + got[2].astype(f32) + got[3].astype(f32)

    part_a = split_sum([part_a[:, r * cols : (r + 1) * cols] for r in range(4)], to_x)
    part_b = split_sum([part_b[i * n : (i + 1) * n] for i in (0, 2, 1, 3)], to_z)
    got = swap_y_lo(jnp.concatenate([part_a[half:], part_b[half:]], 0).astype(bf16))
    grad_input = jnp.concatenate([part_a[:half], part_b[:half]], 0) + got.astype(f32)

    activated = jnp.concatenate([pick(z_hi, back0, back1), pick(z_hi, back1, back0)], 1)

    return (activated, grad_input.astype(bf16), grad_weight)


def solution(mesh):
    placed = (P("ja", ("ka", "ia")), P("ka", ("ia", "ja")), P("ja", ("ia", "ka")))
    return jax.shard_map(
        on_device,
        mesh=mesh,
        in_specs=placed,
        out_specs=(P("ja", ("ia", "ka")), P("ja", ("ka", "ia")), P("ka", ("ia", "ja"))),
        check_vma=False,
    )
```

```python
import jax
import jax.numpy as jnp
from jax import lax
from jax.sharding import PartitionSpec as P

coef_root = 0.7978845608028654
coef_cube = 0.044715
bf16, f32 = jnp.bfloat16, jnp.float32

N_RING = 4
BOTH = ("ja", "ka")


def gelu_pair(hidden):
    tanh_value = jnp.tanh(coef_root * (hidden + coef_cube * hidden * hidden * hidden))
    activ = 0.5 * hidden * (1.0 + tanh_value)
    derivative = 0.5 * (1.0 + tanh_value) + 0.5 * hidden * (
        1.0 - tanh_value * tanh_value
    ) * coef_root * (1.0 + 3.0 * coef_cube * hidden * hidden)
    return (activ, derivative)


def from_x(v, r):
    return lax.ppermute(v, "ia", [((i + r) % N_RING, i) for i in range(N_RING)])


def to_x(v, r):
    return from_x(v, N_RING - r)


def from_z(v, r):
    return lax.ppermute(
        v, "ja", [(y * 4 + (z + r) % N_RING, y * 4 + z) for y in range(2) for z in range(N_RING)]
    )


def to_z(v, r):
    return from_z(v, N_RING - r)


def swap_y_lo(v):
    return lax.ppermute(v, "ja", [(j, j ^ 4) for j in range(8)])


def swap_y_hi(v):
    return lax.ppermute(v, "ka", [(k, k ^ 2) for k in range(4)])


def swap_core(v):
    return lax.ppermute(v, "ka", [(k, k ^ 1) for k in range(4)])


def exchange_pairs(turn):
    pairs = []
    for y_lo in range(2):
        for z in range(4):
            for y_hi in range(2):
                for core in range(2):
                    half = turn ^ (z // 2)
                    to_ja = y_hi * 4 + 2 * core + half
                    to_ka = (y_hi ^ y_lo ^ core) * 2 + ((z % 2) ^ half)
                    pairs.append(((y_lo * 4 + z) * 4 + y_hi * 2 + core, to_ja * 4 + to_ka))
    return pairs


def dot(a, b, dims=(1, 0)):
    return lax.dot_general(
        a, b, (((dims[0],), (dims[1],)), ((), ())), preferred_element_type=f32
    )


def after_done(v, *arrived):
    return lax.optimization_barrier((v, *arrived))[0]


def together(*arrays):
    return lax.optimization_barrier(arrays)


def pick(index, first, second):
    return jnp.where(index == 0, first, second)


def on_device(tokens, weight, grad_out):
    rows, cols = tokens.shape
    half = rows // 2
    units = weight.shape[1]
    x = lax.axis_index("ia")
    z = lax.axis_index("ja") % 4
    z_hi, z_lo = z // 2, z % 2
    y_hi, core = lax.axis_index("ka") // 2, lax.axis_index("ka") % 2
    y_rows = y_hi ^ z_hi

    left, right = grad_out[:, :units], grad_out[:, units:]
    piece0, piece1 = pick(z_hi, left, right), pick(z_hi, right, left)

    other = swap_y_lo(tokens)
    tok_a = jnp.concatenate([tokens[:half], other[:half]], 0)
    tok_b = jnp.concatenate([tokens[half:], other[half:]], 0)
    b2, b1, b3 = (from_z(tok_b, r) for r in (2, 1, 3))
    a2, a1, a3 = (from_x(tok_a, r) for r in (2, 1, 3))
    a0 = jnp.concatenate([tok_a, a1, a2, a3], 1)
    b0 = jnp.concatenate([tok_b, b2, b1, b3], 0)
    n = 2 * half

    held = after_done(weight, a0)
    w = [lax.dynamic_slice_in_dim(held, ((x + r) % N_RING) * cols, cols, 0) for r in range(4)]
    turned = jnp.concatenate(w, 0)
    w = [turned[r * cols : (r + 1) * cols] for r in range(4)]

    sent0 = lax.ppermute(after_done(piece0, a0, b0), BOTH, exchange_pairs(0))
    a1, a3 = from_z(a0, 1), from_z(a0, 3)
    b1, b3 = from_x(b0, 1), from_x(b0, 3)
    a1, a3, b1, b3, sent0 = together(a1, a3, b1, b3, sent0)
    a2_first, a2_second = from_z(a1[:half], 1), from_z(a3[half:], 3)
    b2_first, b2_second = from_x(b1[: 2 * n], 1), from_x(b3[2 * n :], 3)
    early = dot(b0, w[0]) + dot(b1, w[1]) + dot(b3, w[3])
    at_1 = dot(a1, turned)
    sent1 = lax.ppermute(after_done(piece1, at_1), BOTH, exchange_pairs(1))
    a2 = jnp.concatenate([a2_first, a2_second], 0)

    def over_core(first, second):
        got = swap_core(pick(core, second, first).astype(bf16))
        return (pick(core, first, second) + got.astype(f32)).reshape(-1, 2, half, units)

    def over_y(summed, *arrived):
        away = after_done(pick(y_rows, summed[:, 1], summed[:, 0]).astype(bf16), *arrived)
        return pick(y_rows, summed[:, 0], summed[:, 1]) + swap_y_hi(away).astype(f32)

    def gelu(hidden, go):
        activ, derivative = gelu_pair(hidden)
        grad = (go.reshape(hidden.shape).astype(f32) * derivative).astype(bf16)
        return activ.astype(bf16), grad

    def back_core(grad, there):
        grad = jnp.concatenate(
            [v[i] for i in range(grad.shape[0]) for v in (pick(y_rows, grad, there), pick(y_rows, there, grad))], 0
        )
        there = swap_core(grad)
        return pick(core, grad, there), pick(core, there, grad)

    first, second = [dot(a0, turned), dot(a2, turned)], [at_1, dot(a3, turned)]
    summed_a = over_core(jnp.concatenate(first, 0), jnp.concatenate(second, 0))
    summed_b = over_core(
        early[: 2 * n] + dot(b2_first, w[2]), early[2 * n :] + dot(b2_second, w[2])
    )
    summed_a, sent1 = together(summed_a, sent1)
    hidden_a, hidden_b = over_y(summed_a), over_y(summed_b)
    k0 = z_lo ^ z_hi ^ (core & z_lo)
    go0, go1 = pick(k0, sent0, sent1), pick(k0, sent1, sent0)
    act_a, gr_a = gelu(hidden_a, jnp.concatenate([go0[:half], go1[:half]], 0))
    act_b, gr_b = gelu(hidden_b, jnp.concatenate([go0[half:], go1[half:]], 0))
    there_a, there_b = swap_y_hi(gr_a), swap_y_hi(gr_b)

    first, second = back_core(gr_a, there_a)
    g0, g2, g1, g3 = first[:n], first[n:], second[:n], second[n:]
    d2 = dot(g2, turned, (1, 1)).astype(bf16)
    gb0, gb1 = back_core(gr_b, after_done(there_b, d2))

    c2_first, c2_second = dot(gb0, w[2], (1, 1)).astype(bf16), dot(gb1, w[2], (1, 1)).astype(bf16)
    up_a, down_a = to_z(d2[:half], 1), to_z(d2[half:], 3)
    up_b, down_b = to_x(c2_first, 1), to_x(c2_second, 3)

    def before(v, extra):
        return jnp.pad(v, ((0, extra), (0, 0))).astype(f32)

    def after(v, extra):
        return jnp.pad(v, ((extra, 0), (0, 0))).astype(f32)

    gb = jnp.concatenate(together(gb0, gb1, d2, c2_first, c2_second)[:2], 0)
    held0 = jnp.concatenate([act_a[0], act_b[0]], 0)
    held1 = jnp.concatenate([act_a[1], act_b[1]], 0)

    def give_back(turn, *arrived):
        piece = after_done(pick(k0 ^ turn, held0, held1), *arrived)
        return lax.ppermute(piece, BOTH, [(t, s) for s, t in exchange_pairs(turn)])

    back0 = give_back(0, d2, c2_first, c2_second)
    up_a, down_a, up_b, down_b = together(up_a, down_a, up_b, down_b)
    p1, p3 = together(dot(g1, turned, (1, 1)), dot(g3, turned, (1, 1)))
    d1 = (p1 + before(up_a, half)).astype(bf16)
    d3 = (p3 + after(down_a, half)).astype(bf16)
    up_b, down_b, back0 = together(up_b, down_b, back0)
    q1, q3 = together(dot(gb, w[1], (1, 1)), dot(gb, w[3], (1, 1)))
    c1 = (q1 + before(up_b, 2 * n)).astype(bf16)
    c3 = (q3 + after(down_b, 2 * n)).astype(bf16)
    added = (d1, d3, c1, c3)
    d1, d3, c1, c3 = to_z(d1, 1), to_z(d3, 3), to_x(c1, 1), to_x(c3, 3)
    d1, d3, c1, c3 = together(d1, d3, c1, c3)
    part_a = dot(g0, turned, (1, 1)) + d1.astype(f32) + d3.astype(f32)
    part_b = dot(gb, w[0], (1, 1)) + c1.astype(f32) + c3.astype(f32)

    ga = after_done(jnp.concatenate([g0, g1, g2, g3], 0), *added)
    gb = after_done(gb, d1, c1)
    all_a = jnp.concatenate([a0, a1, a2, a3], 0)
    b2 = jnp.concatenate([b2_first, b2_second], 0)
    of_a = lax.optimization_barrier(dot(all_a, ga, (0, 0)))
    blocks = []
    for r, b in enumerate((b0, b1, b2, b3)):
        block = of_a[r * cols : (r + 1) * cols] + dot(b, gb, (0, 0))
        blocks.append(block.astype(bf16))

    back1 = give_back(1, *added)
    grad_weight = jnp.zeros_like(weight)
    for r in range(4):
        grad_weight = lax.dynamic_update_slice_in_dim(
            grad_weight, blocks[r], ((x + r) % N_RING) * cols, 0
        )

    part_a, part_b, back1 = together(part_a, part_b, back1)

    def split_sum(parts, send):
        got = {r: send(parts[r].astype(bf16), r) for r in (2, 1, 3)}
        return parts[0] + got[1].astype(f32) + got[2].astype(f32) + got[3].astype(f32)

    part_a = split_sum([part_a[:, r * cols : (r + 1) * cols] for r in range(4)], to_x)
    part_b = split_sum([part_b[i * n : (i + 1) * n] for i in (0, 2, 1, 3)], to_z)
    got = swap_y_lo(jnp.concatenate([part_a[half:], part_b[half:]], 0).astype(bf16))
    grad_input = jnp.concatenate([part_a[:half], part_b[:half]], 0) + got.astype(f32)

    activated = jnp.concatenate([pick(z_hi, back0, back1), pick(z_hi, back1, back0)], 1)

    return (activated, grad_input.astype(bf16), grad_weight)


def solution(mesh):
    placed = (P("ja", ("ka", "ia")), P("ka", ("ia", "ja")), P("ja", ("ia", "ka")))
    return jax.shard_map(
        on_device,
        mesh=mesh,
        in_specs=placed,
        out_specs=(P("ja", ("ia", "ka")), P("ja", ("ka", "ia")), P("ka", ("ia", "ja"))),
        check_vma=False,
    )
```
